32 devices in a mesh: dp: 2 (over x), expert: 16 (over z, y, core).
Axes of the slice: x: 2, y: 2, z: 4, core: 2. Of those that a mesh axis runs over, the one named last changes fastest.
Arguments:
- preactivations: bfloat16 [512, 8, 1536], P(('dp', 'expert')), may hold values from -6 to 6
- route_weights: float32 [512, 8], P(('dp', 'expert')), may hold values from 0.05 to 0.3
- expert_ids: int32 [512, 8], P(('dp', 'expert')), may hold values from 0 to 15, all different within a row; in each aligned block of 16 rows (0 to 15, 16 to 31, ...) at most 16 rows name the same one
- down_proj: bfloat16 [16, 4096, 768], P('expert'), may hold values from -0.21875 to 0.21875
- output_cotangent: bfloat16 [512, 4096], P(('dp', 'expert')), may hold values from -1.5 to 1.5
Outputs:
- mixed: bfloat16 [512, 4096], P(('dp', 'expert'))
- route_grads: float32 [512, 8], P(('dp', 'expert'))
- pre_grads: bfloat16 [512, 8, 1536], P(('dp', 'expert'))
- down_grads: float32 [16, 4096, 768], P('expert', 'dp')
The draws below stay inside these ranges and needn't reach their ends.
Inputs may be any that keep to these rules, and one draw needn't show every extreme that they name: `expert_ids`: among the 128 slots of one device's tokens, no expert is named more than 16 times, a bound that some block reaches; a token's 8 experts are distinct.
All inputs are finite; a program needn't handle non-finite values.
Results may differ from the reference program's by a relative error of at most 0.017.
Values may be sent and summed in bfloat16 or wider, within the bound.
A program may use at most 64 MiB of HBM per device.

```python
import math
import jax
import jax.numpy as jnp
import numpy as np
from jax import lax

D = 4096
TOP = 8
HID = 768
TOK_DEV = 16
EXPERTS = 16
CAP = 16
TOKENS = 512
N_DP = 2
N_EXPERT = 16


def spiked(result, stream_key, source, target, parts, factor):
    def block_of(axis_at):
        return (jnp.arange(result.shape[axis_at]) // (result.shape[axis_at] // parts)).reshape((-1,) + (1,) * (result.ndim - 1 - axis_at))

    near = jax.random.permutation(stream_key, parts)[block_of(target)]
    far = (block_of(target) + parts // 2) % parts
    return jnp.where((block_of(source) == near) | (block_of(source) == far), factor * result, result)


def block_levels(stream_key, dims, pieces, smallest, high):
    factor_of, own = 1.0, jax.random.fold_in(stream_key, 6)
    for dim, blocks in pieces:
        heights = jnp.exp(jax.random.uniform(jax.random.fold_in(own, dim), (blocks,), jnp.float32, smallest / len(pieces), high / len(pieces)))
        factor_of = factor_of * jnp.repeat(heights, dims[dim] // blocks).reshape([-1 if axis == dim else 1 for axis in range(len(dims))])
    return factor_of


def deal_out(key, own, number, rows, amount, top, most, slope):
    order = jax.random.permutation(key, amount)
    crowded, usual = load_shares(amount, rows * top, most, slope, True), load_shares(amount, rows * top, most, slope, False)
    places = jnp.arange(amount)

    def named(sizes, offset_by):
        used = int((sizes > 0).sum())
        fixed = max(1, used // 4)
        passed = fixed + (places - fixed + offset_by * (used - fixed)) % max(1, amount - fixed)
        return jnp.zeros((amount,), jnp.int32).at[order[jnp.where(places < fixed, places, passed)]].set(jnp.asarray(sizes, jnp.int32))

    sizes = jnp.where(number % 4 == 0, named(crowded, number // 4), named(usual, number - number // 4 - 1))
    mixed = jax.random.permutation(jax.random.fold_in(own, 3), amount)
    source_of, receiver = mixed[0:amount // 2 * 2:2], mixed[1:amount // 2 * 2:2]
    slack = jnp.minimum(sizes[source_of] - 1, most - sizes[receiver]) // 2
    slack = jnp.where((source_of == order[0]) | (receiver == order[0]) | (sizes[receiver] == 0), 0, jnp.maximum(slack, 0))
    passed = jax.random.randint(jax.random.fold_in(own, 4), (amount // 2,), 0, 1 << 20) % (slack + 1)
    sizes = sizes.at[source_of].add(-passed).at[receiver].add(passed)
    labels = jnp.searchsorted(jnp.cumsum(sizes), jnp.arange(rows * top), side="right").astype(jnp.int32)
    listing = labels.reshape(top, rows).T
    listing = listing[jax.random.permutation(jax.random.fold_in(own, 1), rows)]
    offset_by = jax.random.randint(jax.random.fold_in(own, 2), (rows, 1), 0, top)
    return jnp.take_along_axis(listing, (jnp.arange(top)[None, :] + offset_by) % top, axis=1)


def load_shares(count, total, reach, slope, full):
    loads = [(1 << 20) // math.isqrt(grade ** slope) + 1 for grade in range(1, count + 1)]
    largest = reach if full else min(reach, max(-(-total // count), total * loads[0] // sum(loads)))
    least = 1 if total - largest >= count - 1 else 0
    given, spare = [largest] + [least] * (count - 1), total - largest - least * (count - 1)
    while spare > 0:
        free = [i for i in range(1, count) if given[i] < largest] or [i for i in range(1, count) if given[i] < reach]
        mass, budget = sum([loads[i] for i in free]), spare
        for i in free:
            addition = min(reach - given[i], max(1, budget * loads[i] // mass), spare)
            given[i] = given[i] + addition
            spare = spare - addition
    return np.array(given)


def scatter_about(rng, dims, spread, reach, split=(), kind=jnp.bfloat16):
    loudness = block_levels(rng, dims, split, -0.22, 0.18) if split else 1.0
    drawn = jax.random.normal(rng, dims, jnp.float32) * spread * loudness
    return jnp.minimum(jnp.maximum(drawn, -reach), reach).astype(kind)


def heavy_noise(own_key, shape, width, most, cuts, heavy, kind=jnp.bfloat16):
    array = width * jax.random.normal(own_key, shape, jnp.float32)
    if cuts:
        array = array * block_levels(own_key, shape, cuts, -0.22, 0.18)
    return jnp.clip(spiked(array, jax.random.fold_in(own_key, 3), *heavy), -most, most).astype(kind)


def setup_inputs(seed: int = 0) -> dict:
    keys = jax.random.split(jax.random.key(seed), 6)
    preactivations = scatter_about(keys[0], (TOKENS, TOP, 2 * HID), 1.0, 6.0, ((0, 32),))
    route_weights = jnp.clip(0.05 + 0.25 * jax.random.uniform(keys[1], (TOKENS, TOP), jnp.float32) ** block_levels(keys[1], (TOKENS, TOP), ((0, 32),), -0.2, 0.2), 0.05, 0.3)
    expert_ids_keys = jax.random.split(jax.random.fold_in(keys[2], 1), TOKENS // TOK_DEV)
    expert_ids_turns = jax.random.permutation(jax.random.fold_in(keys[2], 3), TOKENS // TOK_DEV)
    expert_ids = jax.vmap(lambda own, number: deal_out(jax.random.fold_in(keys[2], 2), own, number, TOK_DEV, EXPERTS, TOP, CAP, 2))(expert_ids_keys, expert_ids_turns).reshape((TOKENS, TOP))
    down_proj = scatter_about(keys[3], (EXPERTS, D, HID), HID ** -0.5, 0.21875, ((0, 16),))
    output_cotangent = heavy_noise(keys[4], (TOKENS, D), 0.25, 1.5, ((0, 32),), (0, 1, 32, 2.75))
    return dict(preactivations=preactivations, route_weights=route_weights, expert_ids=expert_ids, down_proj=down_proj, output_cotangent=output_cotangent)


def rounded(values):
    return lax.optimization_barrier(values.astype(jnp.bfloat16)).astype(jnp.float32)


def reference(preactivations, route_weights, expert_ids, down_proj, output_cotangent):
    weight = down_proj.astype(jnp.float32)
    slot_count = TOK_DEV * TOP
    pre_all = preactivations.reshape(N_DP, N_EXPERT, slot_count, 2 * HID)
    route_all = route_weights.reshape(N_DP, N_EXPERT, TOK_DEV, TOP)
    ids_all = expert_ids.reshape(N_DP, N_EXPERT, slot_count)
    cot_all = output_cotangent.reshape(N_DP, N_EXPERT, TOK_DEV, D)
    source = jnp.broadcast_to(jnp.arange(N_EXPERT, dtype=jnp.int32)[:, None], (N_EXPERT, slot_count))

    def one_row(running, row_block):
        pre_blk, route_blk, ids_blk, cot_blk = row_block
        pre_vals = pre_blk.astype(jnp.float32)
        gate_pre = pre_vals[..., :HID]
        up_pre = pre_vals[..., HID:]
        sigmoid_gate = jax.nn.sigmoid(gate_pre)
        activated = gate_pre * sigmoid_gate
        hidden = rounded(activated * up_pre)
        cotangent = cot_blk.astype(jnp.float32)
        scaled = rounded(route_blk[..., None] * cotangent[:, :, None, :]).reshape(N_EXPERT, slot_count, D)
        onehot = (ids_blk[..., None] == jnp.arange(EXPERTS, dtype=jnp.int32)).astype(jnp.int32)
        earlier = (jnp.cumsum(onehot, axis=1).astype(jnp.int32) - onehot) * onehot
        slot_rank = jnp.sum(earlier, axis=-1).astype(jnp.int32)
        hidden_buf = jnp.zeros((EXPERTS, N_EXPERT, CAP, HID), jnp.float32).at[ids_blk, source, slot_rank].set(hidden)
        cot_buf = jnp.zeros((EXPERTS, N_EXPERT, CAP, D), jnp.float32).at[ids_blk, source, slot_rank].set(scaled)
        out_buf = rounded(jnp.einsum("escf,edf->escd", hidden_buf, weight))
        grad_buf = rounded(jnp.einsum("escd,edf->escf", cot_buf, weight))
        part_sum = rounded(jnp.einsum("escf,escd->edf", hidden_buf, cot_buf))
        slot_outs = out_buf[ids_blk, source, slot_rank].reshape(N_EXPERT, TOK_DEV, TOP, D)
        slot_grad = grad_buf[ids_blk, source, slot_rank]
        mixed = jnp.einsum("jtk,jtkd->jtd", route_blk, slot_outs).astype(jnp.bfloat16)
        route_grads = jnp.einsum("jtkd,jtd->jtk", slot_outs, cotangent)
        gate_grad = slot_grad * up_pre * (sigmoid_gate * (1.0 + gate_pre * (1.0 - sigmoid_gate)))
        up_grad = slot_grad * activated
        pre_grads = jnp.concatenate([gate_grad, up_grad], axis=-1).astype(jnp.bfloat16)
        return running + part_sum, (mixed, route_grads, pre_grads)

    start_grads = jnp.zeros((EXPERTS, D, HID), jnp.float32)
    down_grads, outputs = lax.scan(one_row, start_grads, (pre_all, route_all, ids_all, cot_all))
    mixed, route_grads, pre_grads = outputs
    mixed = mixed.reshape(TOKENS, D)
    route_grads = route_grads.reshape(TOKENS, TOP)
    pre_grads = pre_grads.reshape(TOKENS, TOP, 2 * HID)
    return mixed, route_grads, pre_grads, down_grads
```

```python
import jax
import jax.numpy as jnp
from jax import lax
from jax.sharding import PartitionSpec as P


def on_device(preactivations, route_weights, expert_ids, down_proj, output_cotangent):
    token_count, per_token, pre_width = preactivations.shape
    hidden_units = pre_width // 2
    model_width = output_cotangent.shape[1]
    experts = lax.axis_size("expert")
    copies = lax.axis_size("dp")
    slot_count = token_count * per_token
    flat_ids = expert_ids.reshape(slot_count)
    slot_token = lax.iota(jnp.int32, slot_count) // per_token
    target = flat_ids * token_count + slot_token
    placement = (
        lax.iota(jnp.int32, experts * token_count)[:, None] == target[None, :]
    ).astype(jnp.bfloat16)
    pre_vals = preactivations.reshape(slot_count, pre_width).astype(jnp.float32)
    gate_pre = pre_vals[:, :hidden_units]
    up_pre = pre_vals[:, hidden_units:]
    sigmoid_gate = jax.nn.sigmoid(gate_pre)
    activated = gate_pre * sigmoid_gate
    hidden = activated * up_pre
    slot_weight = route_weights.reshape(slot_count, 1)
    weighted = (slot_weight * hidden).astype(jnp.bfloat16)
    weight = down_proj[0]

    cot_rows = lax.all_gather(output_cotangent, "expert", axis=0, tiled=True)
    send = jnp.dot(placement, weighted, preferred_element_type=jnp.float32).astype(jnp.bfloat16)
    send = send.reshape(experts, token_count, hidden_units)
    recv = lax.all_to_all(send, "expert", split_axis=0, concat_axis=0, tiled=True)
    hidden_rows = recv.reshape(experts * token_count, hidden_units)

    mixed_part = lax.dot_general(
        hidden_rows, weight, (((1,), (1,)), ((), ())), preferred_element_type=jnp.float32
    ).astype(jnp.bfloat16)
    mixed = lax.psum_scatter(mixed_part, "expert", scatter_dimension=0, tiled=True)

    grad_rows = jnp.dot(cot_rows, weight, preferred_element_type=jnp.float32).astype(jnp.bfloat16)
    grad_back = lax.all_to_all(
        grad_rows.reshape(experts, token_count, hidden_units),
        "expert",
        split_axis=0,
        concat_axis=0,
        tiled=True,
    ).reshape(experts * token_count, hidden_units)

    if copies == 2:
        half = model_width // 2
        mine = lax.axis_index("dp")
        swap = [(0, 1), (1, 0)]
        cot_keep = lax.dynamic_slice_in_dim(cot_rows, mine * half, half, 1)
        cot_give = lax.dynamic_slice_in_dim(cot_rows, (1 - mine) * half, half, 1)
        cot_other = lax.ppermute(cot_give, "dp", swap)
        hidden_other = lax.ppermute(hidden_rows, "dp", swap)
        contract = (((0,), (0,)), ((), ()))
        weight_grads = lax.dot_general(
            cot_keep, hidden_rows, contract, preferred_element_type=jnp.float32
        ) + lax.dot_general(
            cot_other, hidden_other, contract, preferred_element_type=jnp.float32
        )
    else:
        weight_grads = lax.psum_scatter(
            lax.dot_general(
                cot_rows, hidden_rows, (((0,), (0,)), ((), ())), preferred_element_type=jnp.float32
            ).astype(jnp.bfloat16),
            "dp",
            scatter_dimension=0,
            tiled=True,
        ).astype(jnp.float32)

    slot_grad = lax.dot_general(
        placement, grad_back, (((0,), (0,)), ((), ())), preferred_element_type=jnp.float32
    )
    route_grads = jnp.sum(slot_grad * hidden, axis=1).reshape(token_count, per_token)
    hidden_grad = slot_weight * slot_grad
    gate_grad = hidden_grad * up_pre * (sigmoid_gate * (1.0 + gate_pre * (1.0 - sigmoid_gate)))
    up_grad = hidden_grad * activated
    pre_grads = (
        jnp.concatenate([gate_grad, up_grad], axis=1)
        .astype(jnp.bfloat16)
        .reshape(token_count, per_token, pre_width)
    )
    return (mixed, route_grads, pre_grads, weight_grads[None])


def solution(mesh):
    in_specs = (
        P(("dp", "expert"), None, None),
        P(("dp", "expert"), None),
        P(("dp", "expert"), None),
        P("expert", None, None),
        P(("dp", "expert"), None),
    )
    out_specs = (
        P(("dp", "expert"), None),
        P(("dp", "expert"), None),
        P(("dp", "expert"), None, None),
        P("expert", "dp", None),
    )
    return jax.shard_map(
        on_device, mesh=mesh, in_specs=in_specs, out_specs=out_specs, check_vma=False
    )
```

```python
import functools

import jax
import jax.numpy as jnp
from jax import lax
from jax.experimental import pallas as pl
from jax.experimental.pallas import tpu as pltpu
from jax.sharding import PartitionSpec as P

MESH = pl.DeviceIdType.MESH
CHUNKS = 4


def place(n):
    me = lax.axis_index("expert")
    return me, me // 4, (me // 2) % 2, me % 2, n // 4


def greet(n):
    me = lax.axis_index("expert")
    barrier = pltpu.get_barrier_semaphore()
    for step in range(1, n):
        pl.semaphore_signal(
            barrier, inc=1, device_id={"expert": (me + step) % n}, device_id_type=MESH
        )
    pl.semaphore_wait(barrier, n - 1)


def spread_kernel(n, cot_ref, send_ref, cot_all, recv_all, own_sem, *sems):
    far_s, far_r, near_s, near_r, core_s, core_r, swap_s, swap_r = sems
    me, far, near, core, fars = place(n)

    def remote(src, dst, send_sem, recv_sem, target):
        copy = pltpu.make_async_remote_copy(
            src_ref=src,
            dst_ref=dst,
            send_sem=send_sem,
            recv_sem=recv_sem,
            device_id={"expert": target},
            device_id_type=MESH,
        )
        copy.start()
        return copy

    keep_cot = pltpu.make_async_copy(cot_ref, cot_all.at[me], own_sem.at[0])
    keep_row = pltpu.make_async_copy(send_ref.at[me], recv_all.at[me], own_sem.at[1])
    keep_cot.start()
    keep_row.start()
    greet(n)
    sibling = me + 1 - 2 * core
    beside = me + 2 - 4 * near

    far_copies = [
        remote(
            cot_ref,
            cot_all.at[me],
            far_s.at[step - 1],
            far_r.at[step - 1],
            ((far + step) % fars) * 4 + near * 2 + core,
        )
        for step in range(1, fars)
    ]
    near_copies = [remote(cot_ref, cot_all.at[me], near_s.at[0], near_r.at[0], beside)]
    core_copies = [remote(cot_ref, cot_all.at[me], core_s.at[0], core_r.at[0], sibling)]
    swap_copies = []
    for step in range(1, n):
        target = (me + step) % n
        swap_copies.append(
            remote(
                send_ref.at[target],
                recv_all.at[me],
                swap_s.at[step - 1],
                swap_r.at[step - 1],
                target,
            )
        )
    for step in range(1, fars):
        far_copies[step - 1].wait_recv()
        block = ((far - step + fars) % fars) * 4 + near * 2 + core
        ref = cot_all.at[block]
        near_copies.append(remote(ref, ref, near_s.at[step], near_r.at[step], beside))
        core_copies.append(remote(ref, ref, core_s.at[step], core_r.at[step], sibling))
    for step in range(fars):
        near_copies[step].wait_recv()
        block = ((far - step + fars) % fars) * 4 + (1 - near) * 2 + core
        ref = cot_all.at[block]
        at = fars + step
        core_copies.append(remote(ref, ref, core_s.at[at], core_r.at[at], sibling))
    for copy in swap_copies + core_copies:
        copy.wait_recv()
    for copy in far_copies + near_copies + core_copies + swap_copies:
        copy.wait_send()
    keep_cot.wait()
    keep_row.wait()


def spread(cot, send):
    n = lax.axis_size("expert")
    tokens, width = cot.shape
    hidden_units = send.shape[2]
    dma = pltpu.SemaphoreType.DMA
    return pl.pallas_call(
        functools.partial(spread_kernel, n),
        out_shape=(
            jax.ShapeDtypeStruct((n, tokens, width), cot.dtype),
            jax.ShapeDtypeStruct((n, tokens, hidden_units), send.dtype),
        ),
        in_specs=[pl.BlockSpec(memory_space=pltpu.VMEM)] * 2,
        out_specs=[pl.BlockSpec(memory_space=pltpu.VMEM)] * 2,
        scratch_shapes=[dma((2,))]
        + [dma((n // 4 - 1,))] * 2
        + [dma((n // 4,))] * 2
        + [dma((n // 2,))] * 2
        + [dma((n - 1,))] * 2,
        compiler_params=pltpu.CompilerParams(
            collective_id=0, has_side_effects=True, vmem_limit_bytes=32 * 1024 * 1024
        ),
    )(cot, send)


def collect_kernel(n, part_ref, grad_ref, mixed_ref, back_ref, *scratch):
    core_buf, core_sum, near_buf, near_sum, far_buf, own_sem = scratch[:6]
    far_s, far_r, near_s, near_r, core_s, core_r, swap_s, swap_r = scratch[6:]
    me, far, near, core, fars = place(n)
    chunk = core_buf.shape[-1]

    def remote(src, dst, send_sem, recv_sem, target):
        copy = pltpu.make_async_remote_copy(
            src_ref=src,
            dst_ref=dst,
            send_sem=send_sem,
            recv_sem=recv_sem,
            device_id={"expert": target},
            device_id_type=MESH,
        )
        copy.start()
        return copy

    def added(left, right):
        return (left.astype(jnp.float32) + right.astype(jnp.float32)).astype(jnp.bfloat16)

    keep_row = pltpu.make_async_copy(grad_ref.at[me], back_ref.at[me], own_sem.at[0])
    keep_row.start()
    greet(n)
    sibling = me + 1 - 2 * core
    beside = me + 2 - 4 * near
    core_copies = [
        remote(
            part_ref.at[1 - core, :, :, :, pl.ds(at * chunk, chunk)],
            core_buf.at[at],
            core_s.at[at],
            core_r.at[at],
            sibling,
        )
        for at in range(CHUNKS)
    ]
    near_copies, far_copies, swap_copies = [], [], []
    for at in range(CHUNKS):
        core_copies[at].wait_recv()
        mine = part_ref[core, :, :, :, at * chunk : (at + 1) * chunk]
        core_sum[at] = added(mine, core_buf[at])
        near_copies.append(
            remote(
                core_sum.at[at, 1 - near],
                near_buf.at[at],
                near_s.at[at],
                near_r.at[at],
                beside,
            )
        )
    for step in range(1, n):
        target = (me + step) % n
        swap_copies.append(
            remote(
                grad_ref.at[target],
                back_ref.at[me],
                swap_s.at[step - 1],
                swap_r.at[step - 1],
                target,
            )
        )
    for at in range(CHUNKS):
        near_copies[at].wait_recv()
        near_sum[at] = added(core_sum[at, near], near_buf[at])
        for step in range(1, fars):
            target = (far + step) % fars
            slot = at * (fars - 1) + step - 1
            far_copies.append(
                remote(
                    near_sum.at[at, target],
                    far_buf.at[at, step - 1],
                    far_s.at[slot],
                    far_r.at[slot],
                    target * 4 + near * 2 + core,
                )
            )
    for at in range(CHUNKS):
        for step in range(1, fars):
            far_copies[at * (fars - 1) + step - 1].wait_recv()
        total = near_sum[at, far].astype(jnp.float32)
        for step in range(1, fars):
            total = total + far_buf[at, step - 1].astype(jnp.float32)
        mixed_ref[:, at * chunk : (at + 1) * chunk] = total.astype(jnp.bfloat16)
    for copy in swap_copies:
        copy.wait_recv()
    for copy in core_copies + near_copies + far_copies + swap_copies:
        copy.wait_send()
    keep_row.wait()


def collect(part, grad):
    n, tokens, hidden_units = grad.shape
    width = part.shape[-1]
    chunk = width // CHUNKS
    fars = n // 4
    dma = pltpu.SemaphoreType.DMA
    far_count = CHUNKS * (fars - 1)
    return pl.pallas_call(
        functools.partial(collect_kernel, n),
        out_shape=(
            jax.ShapeDtypeStruct((tokens, width), part.dtype),
            jax.ShapeDtypeStruct((n, tokens, hidden_units), grad.dtype),
        ),
        in_specs=[pl.BlockSpec(memory_space=pltpu.VMEM)] * 2,
        out_specs=[pl.BlockSpec(memory_space=pltpu.VMEM)] * 2,
        scratch_shapes=[
            pltpu.VMEM((CHUNKS, 2, fars, tokens, chunk), part.dtype),
            pltpu.VMEM((CHUNKS, 2, fars, tokens, chunk), part.dtype),
            pltpu.VMEM((CHUNKS, fars, tokens, chunk), part.dtype),
            pltpu.VMEM((CHUNKS, fars, tokens, chunk), part.dtype),
            pltpu.VMEM((CHUNKS, fars - 1, tokens, chunk), part.dtype),
            dma((1,)),
        ]
        + [dma((far_count,))] * 2
        + [dma((CHUNKS,))] * 4
        + [dma((n - 1,))] * 2,
        compiler_params=pltpu.CompilerParams(
            collective_id=1, has_side_effects=True, vmem_limit_bytes=32 * 1024 * 1024
        ),
    )(part, grad)


def on_device(preactivations, route_weights, expert_ids, down_proj, output_cotangent):
    token_count, per_token, pre_width = preactivations.shape
    hidden_units = pre_width // 2
    model_width = output_cotangent.shape[1]
    experts = lax.axis_size("expert")
    copies = lax.axis_size("dp")
    slot_count = token_count * per_token
    flat_ids = expert_ids.reshape(slot_count)
    slot_token = lax.iota(jnp.int32, slot_count) // per_token
    target = flat_ids * token_count + slot_token
    placement = (
        lax.iota(jnp.int32, experts * token_count)[:, None] == target[None, :]
    ).astype(jnp.bfloat16)
    pre_vals = preactivations.reshape(slot_count, pre_width).astype(jnp.float32)
    gate_pre = pre_vals[:, :hidden_units]
    up_pre = pre_vals[:, hidden_units:]
    sigmoid_gate = jax.nn.sigmoid(gate_pre)
    activated = gate_pre * sigmoid_gate
    hidden = activated * up_pre
    slot_weight = route_weights.reshape(slot_count, 1)
    weighted = (slot_weight * hidden).astype(jnp.bfloat16)
    weight = down_proj[0]

    send = jnp.dot(placement, weighted, preferred_element_type=jnp.float32).astype(jnp.bfloat16)
    send = send.reshape(experts, token_count, hidden_units)
    by_kernel = copies == 2 and experts % 4 == 0 and experts > 4
    rows = experts * token_count
    if by_kernel:
        cot_rows, recv = spread(output_cotangent, send)
        cot_rows = cot_rows.reshape(rows, model_width)
    else:
        cot_rows = lax.all_gather(output_cotangent, "expert", axis=0, tiled=True)
        recv = lax.all_to_all(send, "expert", split_axis=0, concat_axis=0, tiled=True)
    hidden_rows = recv.reshape(rows, hidden_units)
    grad_rows = (
        jnp.dot(cot_rows, weight, preferred_element_type=jnp.float32)
        .astype(jnp.bfloat16)
        .reshape(experts, token_count, hidden_units)
    )
    across = (((1,), (1,)), ((), ()))
    if by_kernel:
        ordered = recv.reshape(experts // 4, 2, 2, token_count, hidden_units)
        ordered = ordered.transpose(2, 1, 0, 3, 4)
        mixed_part = lax.dot_general(
            ordered.reshape(rows, hidden_units), weight, across, preferred_element_type=jnp.float32
        ).astype(jnp.bfloat16)
        mixed, grad_back = collect(
            mixed_part.reshape(2, 2, experts // 4, token_count, model_width), grad_rows
        )
    else:
        mixed_part = lax.dot_general(
            hidden_rows, weight, across, preferred_element_type=jnp.float32
        ).astype(jnp.bfloat16)
        mixed = lax.psum_scatter(mixed_part, "expert", scatter_dimension=0, tiled=True)
        grad_back = lax.all_to_all(grad_rows, "expert", split_axis=0, concat_axis=0, tiled=True)
    grad_back = grad_back.reshape(rows, hidden_units)

    if copies == 2:
        half = model_width // 2
        mine = lax.axis_index("dp")
        swap = [(0, 1), (1, 0)]
        cot_keep = lax.dynamic_slice_in_dim(cot_rows, mine * half, half, 1)
        cot_give = lax.dynamic_slice_in_dim(cot_rows, (1 - mine) * half, half, 1)
        cot_other = lax.ppermute(cot_give, "dp", swap)
        hidden_other = lax.ppermute(hidden_rows, "dp", swap)
        contract = (((0,), (0,)), ((), ()))
        weight_grads = lax.dot_general(
            cot_keep, hidden_rows, contract, preferred_element_type=jnp.float32
        ) + lax.dot_general(
            cot_other, hidden_other, contract, preferred_element_type=jnp.float32
        )
    else:
        weight_grads = lax.psum_scatter(
            lax.dot_general(
                cot_rows, hidden_rows, (((0,), (0,)), ((), ())), preferred_element_type=jnp.float32
            ).astype(jnp.bfloat16),
            "dp",
            scatter_dimension=0,
            tiled=True,
        ).astype(jnp.float32)

    slot_grad = lax.dot_general(
        placement, grad_back, (((0,), (0,)), ((), ())), preferred_element_type=jnp.float32
    )
    route_grads = jnp.sum(slot_grad * hidden, axis=1).reshape(token_count, per_token)
    hidden_grad = slot_weight * slot_grad
    gate_grad = hidden_grad * up_pre * (sigmoid_gate * (1.0 + gate_pre * (1.0 - sigmoid_gate)))
    up_grad = hidden_grad * activated
    pre_grads = (
        jnp.concatenate([gate_grad, up_grad], axis=1)
        .astype(jnp.bfloat16)
        .reshape(token_count, per_token, pre_width)
    )
    return (mixed, route_grads, pre_grads, weight_grads[None])


def solution(mesh):
    in_specs = (
        P(("dp", "expert"), None, None),
        P(("dp", "expert"), None),
        P(("dp", "expert"), None),
        P("expert", None, None),
        P(("dp", "expert"), None),
    )
    out_specs = (
        P(("dp", "expert"), None),
        P(("dp", "expert"), None),
        P(("dp", "expert"), None, None),
        P("expert", "dp", None),
    )
    return jax.shard_map(
        on_device, mesh=mesh, in_specs=in_specs, out_specs=out_specs, check_vma=False
    )
```

```python
import functools

import jax
import jax.numpy as jnp
from jax import lax
from jax.experimental import pallas as pl
from jax.experimental.pallas import tpu as pltpu
from jax.sharding import PartitionSpec as P

MESH = pl.DeviceIdType.MESH
CHUNKS = 4


def place(n):
    me = lax.axis_index("expert")
    return me, me // 4, (me // 2) % 2, me % 2, n // 4


def greet(n):
    me = lax.axis_index("expert")
    barrier = pltpu.get_barrier_semaphore()
    for step in range(1, n):
        pl.semaphore_signal(
            barrier, inc=1, device_id={"expert": (me + step) % n}, device_id_type=MESH
        )
    pl.semaphore_signal(
        barrier, inc=1, device_id={"dp": 1 - lax.axis_index("dp")}, device_id_type=MESH
    )
    pl.semaphore_wait(barrier, n)


def layer_kernel(
    n,
    cot_ref,
    send_ref,
    weight_ref,
    cot_all,
    recv_all,
    mixed_ref,
    back_ref,
    cot_far,
    recv_far,
    *scratch,
):
    held, part, grad, core_buf, core_sum, near_buf, near_sum, far_buf = scratch[:8]
    own_sem, far_s, far_r, near_s, near_r, core_s, core_r, swap_s, swap_r = scratch[8:17]
    ofar_s, ofar_r, onear_s, onear_r, ocore_s, ocore_r, oswap_s, oswap_r = scratch[17:25]
    pair_s, pair_r, pass_s, pass_r = scratch[25:]
    me, far, near, core, fars = place(n)
    tokens, width = cot_ref.shape
    hidden_units = send_ref.shape[-1]
    chunk = width // CHUNKS

    def remote(src, dst, send_sem, recv_sem, target):
        copy = pltpu.make_async_remote_copy(
            src_ref=src,
            dst_ref=dst,
            send_sem=send_sem,
            recv_sem=recv_sem,
            device_id={"expert": target},
            device_id_type=MESH,
        )
        copy.start()
        return copy

    half = width // 2
    other = 1 - lax.axis_index("dp")
    columns_there = pl.ds(pl.multiple_of(other * half, half), half)

    def pair(src, dst, at):
        copy = pltpu.make_async_remote_copy(
            src_ref=src,
            dst_ref=dst,
            send_sem=pair_s.at[at],
            recv_sem=pair_r.at[at],
            device_id={"dp": other},
            device_id_type=MESH,
        )
        copy.start()
        return copy

    def added(left, right):
        return (left.astype(jnp.float32) + right.astype(jnp.float32)).astype(jnp.bfloat16)

    keep_cot = pltpu.make_async_copy(cot_ref, cot_all.at[me], own_sem.at[0])
    keep_row = pltpu.make_async_copy(send_ref.at[me], recv_all.at[me], own_sem.at[1])
    load = pltpu.make_async_copy(weight_ref, held, own_sem.at[2])
    keep_cot.start()
    keep_row.start()
    load.start()
    greet(n)
    sibling = me + 1 - 2 * core
    beside = me + 2 - 4 * near

    swap_copies = []
    for step in range(1, n):
        target = (me + step) % n
        swap_copies.append(
            remote(
                send_ref.at[target],
                recv_all.at[me],
                swap_s.at[step - 1],
                swap_r.at[step - 1],
                target,
            )
        )
    far_copies = [
        remote(
            cot_ref,
            cot_all.at[me],
            far_s.at[step - 1],
            far_r.at[step - 1],
            ((far + step) % fars) * 4 + near * 2 + core,
        )
        for step in range(1, fars)
    ]
    near_copies = [remote(cot_ref, cot_all.at[me], near_s.at[0], near_r.at[0], beside)]
    core_copies = [remote(cot_ref, cot_all.at[me], core_s.at[0], core_r.at[0], sibling)]
    blocks = [me]
    pairs = [pair(cot_ref.at[:, columns_there], cot_far.at[me], 0)]
    for step in range(1, fars):
        far_copies[step - 1].wait_recv()
        block = ((far - step + fars) % fars) * 4 + near * 2 + core
        ref = cot_all.at[block]
        near_copies.append(remote(ref, ref, near_s.at[step], near_r.at[step], beside))
        core_copies.append(remote(ref, ref, core_s.at[step], core_r.at[step], sibling))
        pairs.append(pair(ref.at[:, columns_there], cot_far.at[block], step))
        blocks.append(block)

    for copy in swap_copies:
        copy.wait_recv()
    keep_row.wait()
    row_pair = pair(recv_all, recv_far, 2 * fars)
    load.wait()
    hidden = recv_all[...].reshape(n * tokens, hidden_units)
    ocore = []
    for at in range(CHUNKS):
        out = lax.dot_general(
            hidden,
            held[at * chunk : (at + 1) * chunk, :],
            (((1,), (1,)), ((), ())),
            preferred_element_type=jnp.float32,
        )
        part[at] = out.astype(jnp.bfloat16).reshape(fars, 2, 2, tokens, chunk)
        ocore.append(
            remote(
                part.at[at, :, :, 1 - core],
                core_buf.at[at],
                ocore_s.at[at],
                ocore_r.at[at],
                sibling,
            )
        )

    for step in range(fars):
        near_copies[step].wait_recv()
        block = ((far - step + fars) % fars) * 4 + (1 - near) * 2 + core
        ref = cot_all.at[block]
        at = fars + step
        core_copies.append(remote(ref, ref, core_s.at[at], core_r.at[at], sibling))
        pairs.append(pair(ref.at[:, columns_there], cot_far.at[block], at))
        blocks.append(block)

    onear = []
    for at in range(CHUNKS):
        ocore[at].wait_recv()
        core_sum[at] = added(part[at, :, :, core], core_buf[at])
        onear.append(
            remote(
                core_sum.at[at, :, 1 - near],
                near_buf.at[at],
                onear_s.at[at],
                onear_r.at[at],
                beside,
            )
        )

    for copy in core_copies:
        copy.wait_recv()
    keep_cot.wait()
    tile = hidden_units // 3 if hidden_units % 384 == 0 else hidden_units

    @pl.loop(0, hidden_units // tile)
    def _(at):
        columns = pl.ds(pl.multiple_of(at * tile, tile), tile)
        found = jnp.dot(
            cot_all[...].reshape(n * tokens, width),
            held[:, columns],
            preferred_element_type=jnp.float32,
        )
        grad[:, :, columns] = found.astype(jnp.bfloat16).reshape(n, tokens, tile)

    keep_grad = pltpu.make_async_copy(grad.at[me], back_ref.at[me], own_sem.at[3])
    keep_grad.start()
    oswap = []
    for step in range(1, n):
        target = (me + step) % n
        oswap.append(
            remote(
                grad.at[target],
                back_ref.at[me],
                oswap_s.at[step - 1],
                oswap_r.at[step - 1],
                target,
            )
        )
    ofar = []
    for at in range(CHUNKS):
        onear[at].wait_recv()
        near_sum[at] = added(core_sum[at, :, near], near_buf[at])
        for step in range(1, fars):
            target = (far + step) % fars
            slot = at * (fars - 1) + step - 1
            ofar.append(
                remote(
                    near_sum.at[at, target],
                    far_buf.at[at, step - 1],
                    ofar_s.at[slot],
                    ofar_r.at[slot],
                    target * 4 + near * 2 + core,
                )
            )
    for at in range(CHUNKS):
        for step in range(1, fars):
            ofar[at * (fars - 1) + step - 1].wait_recv()
        total = near_sum[at, far].astype(jnp.float32)
        for step in range(1, fars):
            total = total + far_buf[at, step - 1].astype(jnp.float32)
        mixed_ref[:, at * chunk : (at + 1) * chunk] = total.astype(jnp.bfloat16)
    passes = []
    for at in range(2 * fars):
        pairs[at].wait_recv()
        ref = cot_far.at[blocks[at]]
        passes.append(remote(ref, ref, pass_s.at[at], pass_r.at[at], sibling))
    for copy in oswap + passes + [row_pair]:
        copy.wait_recv()
    for copy in far_copies + near_copies + core_copies + swap_copies:
        copy.wait_send()
    for copy in ocore + onear + ofar + oswap + pairs + passes + [row_pair]:
        copy.wait_send()
    keep_grad.wait()


def layer(cot, send, weight):
    n, tokens, hidden_units = send.shape
    width = cot.shape[1]
    chunk = width // CHUNKS
    fars = n // 4
    kind = cot.dtype
    dma = pltpu.SemaphoreType.DMA
    in_vmem = pl.BlockSpec(memory_space=pltpu.VMEM)
    return pl.pallas_call(
        functools.partial(layer_kernel, n),
        out_shape=(
            jax.ShapeDtypeStruct((n, tokens, width), kind),
            jax.ShapeDtypeStruct((n, tokens, hidden_units), kind),
            jax.ShapeDtypeStruct((tokens, width), kind),
            jax.ShapeDtypeStruct((n, tokens, hidden_units), kind),
            jax.ShapeDtypeStruct((n, tokens, width // 2), kind),
            jax.ShapeDtypeStruct((n, tokens, hidden_units), kind),
        ),
        in_specs=[in_vmem, in_vmem, pl.BlockSpec(memory_space=pltpu.HBM)],
        out_specs=[in_vmem] * 6,
        scratch_shapes=[
            pltpu.VMEM(weight.shape, kind),
            pltpu.VMEM((CHUNKS, fars, 2, 2, tokens, chunk), kind),
            pltpu.VMEM((n, tokens, hidden_units), kind),
            pltpu.VMEM((CHUNKS, fars, 2, tokens, chunk), kind),
            pltpu.VMEM((CHUNKS, fars, 2, tokens, chunk), kind),
            pltpu.VMEM((CHUNKS, fars, tokens, chunk), kind),
            pltpu.VMEM((CHUNKS, fars, tokens, chunk), kind),
            pltpu.VMEM((CHUNKS, fars - 1, tokens, chunk), kind),
            dma((4,)),
        ]
        + [dma((fars - 1,))] * 2
        + [dma((fars,))] * 2
        + [dma((2 * fars,))] * 2
        + [dma((n - 1,))] * 2
        + [dma((CHUNKS * (fars - 1),))] * 2
        + [dma((CHUNKS,))] * 4
        + [dma((n - 1,))] * 2
        + [dma((2 * fars + 1,))] * 2
        + [dma((2 * fars,))] * 2,
        compiler_params=pltpu.CompilerParams(
            collective_id=0, has_side_effects=True, vmem_limit_bytes=40 * 1024 * 1024
        ),
    )(cot, send, weight)


def on_device(preactivations, route_weights, expert_ids, down_proj, output_cotangent):
    token_count, per_token, pre_width = preactivations.shape
    hidden_units = pre_width // 2
    model_width = output_cotangent.shape[1]
    experts = lax.axis_size("expert")
    copies = lax.axis_size("dp")
    slot_count = token_count * per_token
    flat_ids = expert_ids.reshape(slot_count)
    slot_token = lax.iota(jnp.int32, slot_count) // per_token
    target = flat_ids * token_count + slot_token
    placement = (
        lax.iota(jnp.int32, experts * token_count)[:, None] == target[None, :]
    ).astype(jnp.bfloat16)
    pre_vals = preactivations.reshape(slot_count, pre_width).astype(jnp.float32)
    gate_pre = pre_vals[:, :hidden_units]
    up_pre = pre_vals[:, hidden_units:]
    sigmoid_gate = jax.nn.sigmoid(gate_pre)
    activated = gate_pre * sigmoid_gate
    hidden = activated * up_pre
    slot_weight = route_weights.reshape(slot_count, 1)
    weighted = (slot_weight * hidden).astype(jnp.bfloat16)
    weight = down_proj[0]

    send = jnp.dot(placement, weighted, preferred_element_type=jnp.float32).astype(jnp.bfloat16)
    send = send.reshape(experts, token_count, hidden_units)
    by_kernel = copies == 2 and experts % 4 == 0 and experts > 4
    rows = experts * token_count
    if by_kernel:
        cot_rows, recv, mixed, grad_back, cot_other, hidden_other = layer(
            output_cotangent, send, weight
        )
        cot_other = cot_other.reshape(rows, model_width // 2)
        hidden_other = hidden_other.reshape(rows, hidden_units)
        cot_rows = cot_rows.reshape(rows, model_width)
        hidden_rows = recv.reshape(rows, hidden_units)
    else:
        cot_rows = lax.all_gather(output_cotangent, "expert", axis=0, tiled=True)
        recv = lax.all_to_all(send, "expert", split_axis=0, concat_axis=0, tiled=True)
        hidden_rows = recv.reshape(rows, hidden_units)
        grad_rows = (
            jnp.dot(cot_rows, weight, preferred_element_type=jnp.float32)
            .astype(jnp.bfloat16)
            .reshape(experts, token_count, hidden_units)
        )
        mixed_part = lax.dot_general(
            hidden_rows, weight, (((1,), (1,)), ((), ())), preferred_element_type=jnp.float32
        ).astype(jnp.bfloat16)
        mixed = lax.psum_scatter(mixed_part, "expert", scatter_dimension=0, tiled=True)
        grad_back = lax.all_to_all(grad_rows, "expert", split_axis=0, concat_axis=0, tiled=True)
    grad_back = grad_back.reshape(rows, hidden_units)

    if by_kernel:
        half = model_width // 2
        cot_keep = lax.dynamic_slice_in_dim(cot_rows, lax.axis_index("dp") * half, half, 1)
        contract = (((0,), (0,)), ((), ()))
        weight_grads = lax.dot_general(
            cot_keep, hidden_rows, contract, preferred_element_type=jnp.float32
        ) + lax.dot_general(
            cot_other, hidden_other, contract, preferred_element_type=jnp.float32
        )
    else:
        weight_grads = lax.psum_scatter(
            lax.dot_general(
                cot_rows, hidden_rows, (((0,), (0,)), ((), ())), preferred_element_type=jnp.float32
            ).astype(jnp.bfloat16),
            "dp",
            scatter_dimension=0,
            tiled=True,
        ).astype(jnp.float32)

    slot_grad = lax.dot_general(
        placement, grad_back, (((0,), (0,)), ((), ())), preferred_element_type=jnp.float32
    )
    route_grads = jnp.sum(slot_grad * hidden, axis=1).reshape(token_count, per_token)
    hidden_grad = slot_weight * slot_grad
    gate_grad = hidden_grad * up_pre * (sigmoid_gate * (1.0 + gate_pre * (1.0 - sigmoid_gate)))
    up_grad = hidden_grad * activated
    pre_grads = (
        jnp.concatenate([gate_grad, up_grad], axis=1)
        .astype(jnp.bfloat16)
        .reshape(token_count, per_token, pre_width)
    )
    return (mixed, route_grads, pre_grads, weight_grads[None])


def solution(mesh):
    in_specs = (
        P(("dp", "expert"), None, None),
        P(("dp", "expert"), None),
        P(("dp", "expert"), None),
        P("expert", None, None),
        P(("dp", "expert"), None),
    )
    out_specs = (
        P(("dp", "expert"), None),
        P(("dp", "expert"), None),
        P(("dp", "expert"), None, None),
        P("expert", "dp", None),
    )
    return jax.shard_map(
        on_device, mesh=mesh, in_specs=in_specs, out_specs=out_specs, check_vma=False
    )
```

```python
import functools

import jax
import jax.numpy as jnp
from jax import lax
from jax.experimental import pallas as pl
from jax.experimental.pallas import tpu as pltpu
from jax.sharding import PartitionSpec as P

MESH = pl.DeviceIdType.MESH
CHUNKS = 4


def place(n):
    me = lax.axis_index("expert")
    return me, me // 4, (me // 2) % 2, me % 2, n // 4


def greet(n):
    me = lax.axis_index("expert")
    barrier = pltpu.get_barrier_semaphore()
    for step in range(1, n):
        pl.semaphore_signal(
            barrier, inc=1, device_id={"expert": (me + step) % n}, device_id_type=MESH
        )
    pl.semaphore_signal(
        barrier, inc=1, device_id={"dp": 1 - lax.axis_index("dp")}, device_id_type=MESH
    )
    pl.semaphore_wait(barrier, n)


def layer_kernel(
    n,
    cot_ref,
    send_ref,
    weight_ref,
    cot_all,
    recv_all,
    mixed_ref,
    back_ref,
    cot_far,
    recv_far,
    *scratch,
):
    held, part, grad, core_buf, core_sum, near_buf, near_sum, far_buf = scratch[:8]
    own_sem, far_s, far_r, near_s, near_r, core_s, core_r, swap_s, swap_r = scratch[8:17]
    ofar_s, ofar_r, onear_s, onear_r, ocore_s, ocore_r, oswap_s, oswap_r = scratch[17:25]
    pair_s, pair_r, pass_s, pass_r = scratch[25:]
    me, far, near, core, fars = place(n)
    tokens, width = cot_ref.shape
    hidden_units = send_ref.shape[-1]
    chunk = width // CHUNKS

    def remote(src, dst, send_sem, recv_sem, target):
        copy = pltpu.make_async_remote_copy(
            src_ref=src,
            dst_ref=dst,
            send_sem=send_sem,
            recv_sem=recv_sem,
            device_id={"expert": target},
            device_id_type=MESH,
        )
        copy.start()
        return copy

    half = width // 2
    other = 1 - lax.axis_index("dp")
    columns_there = pl.ds(pl.multiple_of(other * half, half), half)

    def pair(src, dst, at):
        copy = pltpu.make_async_remote_copy(
            src_ref=src,
            dst_ref=dst,
            send_sem=pair_s.at[at],
            recv_sem=pair_r.at[at],
            device_id={"dp": other},
            device_id_type=MESH,
        )
        copy.start()
        return copy

    def added(left, right):
        return (left.astype(jnp.float32) + right.astype(jnp.float32)).astype(jnp.bfloat16)

    keep_cot = pltpu.make_async_copy(cot_ref, cot_all.at[me], own_sem.at[0])
    keep_row = pltpu.make_async_copy(send_ref.at[me], recv_all.at[me], own_sem.at[1])
    load = pltpu.make_async_copy(weight_ref, held, own_sem.at[2])
    keep_cot.start()
    keep_row.start()
    load.start()
    greet(n)
    sibling = me + 1 - 2 * core
    beside = me + 2 - 4 * near

    swap_copies = []
    for step in range(1, n):
        target = (me + step) % n
        swap_copies.append(
            remote(
                send_ref.at[target],
                recv_all.at[me],
                swap_s.at[step - 1],
                swap_r.at[step - 1],
                target,
            )
        )
    far_copies = [
        remote(
            cot_ref,
            cot_all.at[me],
            far_s.at[step - 1],
            far_r.at[step - 1],
            ((far + step) % fars) * 4 + near * 2 + core,
        )
        for step in range(1, fars)
    ]
    near_copies = [remote(cot_ref, cot_all.at[me], near_s.at[0], near_r.at[0], beside)]
    core_copies = [remote(cot_ref, cot_all.at[me], core_s.at[0], core_r.at[0], sibling)]
    blocks = [me]
    pairs = [pair(cot_ref.at[:, columns_there], cot_far.at[me], 0)]
    for step in range(1, fars):
        far_copies[step - 1].wait_recv()
        block = ((far - step + fars) % fars) * 4 + near * 2 + core
        ref = cot_all.at[block]
        near_copies.append(remote(ref, ref, near_s.at[step], near_r.at[step], beside))
        core_copies.append(remote(ref, ref, core_s.at[step], core_r.at[step], sibling))
        pairs.append(pair(ref.at[:, columns_there], cot_far.at[block], step))
        blocks.append(block)

    for copy in swap_copies:
        copy.wait_recv()
    keep_row.wait()
    row_pair = pair(recv_all, recv_far, 2 * fars)
    load.wait()
    hidden = recv_all[...].reshape(n * tokens, hidden_units)
    ocore = []
    for at in range(CHUNKS):
        out = lax.dot_general(
            hidden,
            held[at * chunk : (at + 1) * chunk, :],
            (((1,), (1,)), ((), ())),
            preferred_element_type=jnp.float32,
        )
        part[at] = out.astype(jnp.bfloat16).reshape(fars, 2, 2, tokens, chunk)
        ocore.append(
            remote(
                part.at[at, :, :, 1 - core],
                core_buf.at[at],
                ocore_s.at[at],
                ocore_r.at[at],
                sibling,
            )
        )

    for step in range(fars):
        near_copies[step].wait_recv()
        block = ((far - step + fars) % fars) * 4 + (1 - near) * 2 + core
        ref = cot_all.at[block]
        at = fars + step
        core_copies.append(remote(ref, ref, core_s.at[at], core_r.at[at], sibling))
        pairs.append(pair(ref.at[:, columns_there], cot_far.at[block], at))
        blocks.append(block)

    onear = []
    for at in range(CHUNKS):
        ocore[at].wait_recv()
        core_sum[at] = added(part[at, :, :, core], core_buf[at])
        onear.append(
            remote(
                core_sum.at[at, :, 1 - near],
                near_buf.at[at],
                onear_s.at[at],
                onear_r.at[at],
                beside,
            )
        )

    for copy in core_copies:
        copy.wait_recv()
    keep_cot.wait()
    tile = hidden_units // 3 if hidden_units % 384 == 0 else hidden_units

    @pl.loop(0, hidden_units // tile)
    def _(at):
        columns = pl.ds(pl.multiple_of(at * tile, tile), tile)
        found = jnp.dot(
            cot_all[...].reshape(n * tokens, width),
            held[:, columns],
            preferred_element_type=jnp.float32,
        )
        grad[:, :, columns] = found.astype(jnp.bfloat16).reshape(n, tokens, tile)

    keep_grad = pltpu.make_async_copy(grad.at[me], back_ref.at[me], own_sem.at[3])
    keep_grad.start()
    oswap = []
    for step in range(1, n):
        target = (me + step) % n
        oswap.append(
            remote(
                grad.at[target],
                back_ref.at[me],
                oswap_s.at[step - 1],
                oswap_r.at[step - 1],
                target,
            )
        )
    ofar = []
    for at in range(CHUNKS):
        onear[at].wait_recv()
        near_sum[at] = added(core_sum[at, :, near], near_buf[at])
        for step in range(1, fars):
            target = (far + step) % fars
            slot = at * (fars - 1) + step - 1
            ofar.append(
                remote(
                    near_sum.at[at, target],
                    far_buf.at[at, step - 1],
                    ofar_s.at[slot],
                    ofar_r.at[slot],
                    target * 4 + near * 2 + core,
                )
            )
    for at in range(CHUNKS):
        for step in range(1, fars):
            ofar[at * (fars - 1) + step - 1].wait_recv()
        total = near_sum[at, far].astype(jnp.float32)
        for step in range(1, fars):
            total = total + far_buf[at, step - 1].astype(jnp.float32)
        mixed_ref[:, at * chunk : (at + 1) * chunk] = total.astype(jnp.bfloat16)
    passes = []
    for at in range(2 * fars):
        pairs[at].wait_recv()
        ref = cot_far.at[blocks[at]]
        passes.append(remote(ref, ref, pass_s.at[at], pass_r.at[at], sibling))
    for copy in oswap + passes + [row_pair]:
        copy.wait_recv()
    for copy in far_copies + near_copies + core_copies + swap_copies:
        copy.wait_send()
    for copy in ocore + onear + ofar + oswap + pairs + passes + [row_pair]:
        copy.wait_send()
    keep_grad.wait()


def layer(cot, send, weight):
    n, tokens, hidden_units = send.shape
    width = cot.shape[1]
    chunk = width // CHUNKS
    fars = n // 4
    kind = cot.dtype
    dma = pltpu.SemaphoreType.DMA
    in_vmem = pl.BlockSpec(memory_space=pltpu.VMEM)
    return pl.pallas_call(
        functools.partial(layer_kernel, n),
        out_shape=(
            jax.ShapeDtypeStruct((n, tokens, width), kind),
            jax.ShapeDtypeStruct((n, tokens, hidden_units), kind),
            jax.ShapeDtypeStruct((tokens, width), kind),
            jax.ShapeDtypeStruct((n, tokens, hidden_units), kind),
            jax.ShapeDtypeStruct((n, tokens, width // 2), kind),
            jax.ShapeDtypeStruct((n, tokens, hidden_units), kind),
        ),
        in_specs=[in_vmem, in_vmem, pl.BlockSpec(memory_space=pltpu.HBM)],
        out_specs=[in_vmem] * 6,
        scratch_shapes=[
            pltpu.VMEM(weight.shape, kind),
            pltpu.VMEM((CHUNKS, fars, 2, 2, tokens, chunk), kind),
            pltpu.VMEM((n, tokens, hidden_units), kind),
            pltpu.VMEM((CHUNKS, fars, 2, tokens, chunk), kind),
            pltpu.VMEM((CHUNKS, fars, 2, tokens, chunk), kind),
            pltpu.VMEM((CHUNKS, fars, tokens, chunk), kind),
            pltpu.VMEM((CHUNKS, fars, tokens, chunk), kind),
            pltpu.VMEM((CHUNKS, fars - 1, tokens, chunk), kind),
            dma((4,)),
        ]
        + [dma((fars - 1,))] * 2
        + [dma((fars,))] * 2
        + [dma((2 * fars,))] * 2
        + [dma((n - 1,))] * 2
        + [dma((CHUNKS * (fars - 1),))] * 2
        + [dma((CHUNKS,))] * 4
        + [dma((n - 1,))] * 2
        + [dma((2 * fars + 1,))] * 2
        + [dma((2 * fars,))] * 2,
        compiler_params=pltpu.CompilerParams(
            collective_id=0, has_side_effects=True, vmem_limit_bytes=54 * 1024 * 1024
        ),
    )(cot, send, weight)


def on_device(preactivations, route_weights, expert_ids, down_proj, output_cotangent):
    token_count, per_token, pre_width = preactivations.shape
    hidden_units = pre_width // 2
    model_width = output_cotangent.shape[1]
    experts = lax.axis_size("expert")
    copies = lax.axis_size("dp")
    slot_count = token_count * per_token
    flat_ids = expert_ids.reshape(slot_count)
    slot_token = lax.iota(jnp.int32, slot_count) // per_token
    target = flat_ids * token_count + slot_token
    placement = (
        lax.iota(jnp.int32, experts * token_count)[:, None] == target[None, :]
    ).astype(jnp.bfloat16)
    pre_vals = preactivations.reshape(slot_count, pre_width).astype(jnp.float32)
    gate_pre = pre_vals[:, :hidden_units]
    up_pre = pre_vals[:, hidden_units:]
    sigmoid_gate = jax.nn.sigmoid(gate_pre)
    activated = gate_pre * sigmoid_gate
    hidden = activated * up_pre
    slot_weight = route_weights.reshape(slot_count, 1)
    weighted = (slot_weight * hidden).astype(jnp.bfloat16)
    weight = down_proj[0]

    send = jnp.dot(placement, weighted, preferred_element_type=jnp.float32).astype(jnp.bfloat16)
    send = send.reshape(experts, token_count, hidden_units)
    by_kernel = copies == 2 and experts % 4 == 0 and experts > 4
    rows = experts * token_count
    if by_kernel:
        cot_rows, recv, mixed, grad_back, cot_other, hidden_other = layer(
            output_cotangent, send, weight
        )
        cot_other = cot_other.reshape(rows, model_width // 2)
        hidden_other = hidden_other.reshape(rows, hidden_units)
        cot_rows = cot_rows.reshape(rows, model_width)
        hidden_rows = recv.reshape(rows, hidden_units)
    else:
        cot_rows = lax.all_gather(output_cotangent, "expert", axis=0, tiled=True)
        recv = lax.all_to_all(send, "expert", split_axis=0, concat_axis=0, tiled=True)
        hidden_rows = recv.reshape(rows, hidden_units)
        grad_rows = (
            jnp.dot(cot_rows, weight, preferred_element_type=jnp.float32)
            .astype(jnp.bfloat16)
            .reshape(experts, token_count, hidden_units)
        )
        mixed_part = lax.dot_general(
            hidden_rows, weight, (((1,), (1,)), ((), ())), preferred_element_type=jnp.float32
        ).astype(jnp.bfloat16)
        mixed = lax.psum_scatter(mixed_part, "expert", scatter_dimension=0, tiled=True)
        grad_back = lax.all_to_all(grad_rows, "expert", split_axis=0, concat_axis=0, tiled=True)
    grad_back = grad_back.reshape(rows, hidden_units)

    if by_kernel:
        half = model_width // 2
        cot_keep = lax.dynamic_slice_in_dim(cot_rows, lax.axis_index("dp") * half, half, 1)
        contract = (((0,), (0,)), ((), ()))
        weight_grads = lax.dot_general(
            cot_keep, hidden_rows, contract, preferred_element_type=jnp.float32
        ) + lax.dot_general(
            cot_other, hidden_other, contract, preferred_element_type=jnp.float32
        )
    else:
        weight_grads = lax.psum_scatter(
            lax.dot_general(
                cot_rows, hidden_rows, (((0,), (0,)), ((), ())), preferred_element_type=jnp.float32
            ).astype(jnp.bfloat16),
            "dp",
            scatter_dimension=0,
            tiled=True,
        ).astype(jnp.float32)

    slot_grad = lax.dot_general(
        placement, grad_back, (((0,), (0,)), ((), ())), preferred_element_type=jnp.float32
    )
    route_grads = jnp.sum(slot_grad * hidden, axis=1).reshape(token_count, per_token)
    hidden_grad = slot_weight * slot_grad
    gate_grad = hidden_grad * up_pre * (sigmoid_gate * (1.0 + gate_pre * (1.0 - sigmoid_gate)))
    up_grad = hidden_grad * activated
    pre_grads = (
        jnp.concatenate([gate_grad, up_grad], axis=1)
        .astype(jnp.bfloat16)
        .reshape(token_count, per_token, pre_width)
    )
    return (mixed, route_grads, pre_grads, weight_grads[None])


def solution(mesh):
    in_specs = (
        P(("dp", "expert"), None, None),
        P(("dp", "expert"), None),
        P(("dp", "expert"), None),
        P("expert", None, None),
        P(("dp", "expert"), None),
    )
    out_specs = (
        P(("dp", "expert"), None),
        P(("dp", "expert"), None),
        P(("dp", "expert"), None, None),
        P("expert", "dp", None),
    )
    return jax.shard_map(
        on_device, mesh=mesh, in_specs=in_specs, out_specs=out_specs, check_vma=False
    )
```

```python
import functools

import jax
import jax.numpy as jnp
from jax import lax
from jax.experimental import pallas as pl
from jax.experimental.pallas import tpu as pltpu
from jax.sharding import PartitionSpec as P

MESH = pl.DeviceIdType.MESH
CHUNKS = 4


def place(n):
    me = lax.axis_index("expert")
    return me, me // 4, (me // 2) % 2, me % 2, n // 4


def greet(n):
    me = lax.axis_index("expert")
    barrier = pltpu.get_barrier_semaphore()
    for step in range(1, n):
        pl.semaphore_signal(
            barrier, inc=1, device_id={"expert": (me + step) % n}, device_id_type=MESH
        )
    pl.semaphore_signal(
        barrier, inc=1, device_id={"dp": 1 - lax.axis_index("dp")}, device_id_type=MESH
    )
    pl.semaphore_wait(barrier, n)


def layer_kernel(
    n,
    cot_ref,
    send_ref,
    weight_ref,
    cot_all,
    recv_all,
    mixed_ref,
    back_ref,
    cot_far,
    recv_far,
    *scratch,
):
    held, part, grad, core_buf, core_sum, near_buf, near_sum, far_buf = scratch[:8]
    own_sem, far_s, far_r, near_s, near_r, core_s, core_r, swap_s, swap_r = scratch[8:17]
    ofar_s, ofar_r, onear_s, onear_r, ocore_s, ocore_r, oswap_s, oswap_r = scratch[17:25]
    pair_s, pair_r, pass_s, pass_r = scratch[25:]
    me, far, near, core, fars = place(n)
    tokens, width = cot_ref.shape
    hidden_units = send_ref.shape[-1]
    chunk = width // CHUNKS

    def remote(src, dst, send_sem, recv_sem, target):
        copy = pltpu.make_async_remote_copy(
            src_ref=src,
            dst_ref=dst,
            send_sem=send_sem,
            recv_sem=recv_sem,
            device_id={"expert": target},
            device_id_type=MESH,
        )
        copy.start()
        return copy

    half = width // 2
    other = 1 - lax.axis_index("dp")
    columns_there = pl.ds(pl.multiple_of(other * half, half), half)

    def pair(src, dst, at):
        copy = pltpu.make_async_remote_copy(
            src_ref=src,
            dst_ref=dst,
            send_sem=pair_s.at[at],
            recv_sem=pair_r.at[at],
            device_id={"dp": other},
            device_id_type=MESH,
        )
        copy.start()
        return copy

    def added(left, right):
        return (left.astype(jnp.float32) + right.astype(jnp.float32)).astype(jnp.bfloat16)

    keep_cot = pltpu.make_async_copy(cot_ref, cot_all.at[me], own_sem.at[0])
    keep_row = pltpu.make_async_copy(send_ref.at[me], recv_all.at[me], own_sem.at[1])
    load = pltpu.make_async_copy(weight_ref, held, own_sem.at[2])
    keep_cot.start()
    keep_row.start()
    load.start()
    greet(n)
    sibling = me + 1 - 2 * core
    beside = me + 2 - 4 * near

    swap_copies = []
    for step in range(1, n):
        target = (me + step) % n
        swap_copies.append(
            remote(
                send_ref.at[target],
                recv_all.at[me],
                swap_s.at[step - 1],
                swap_r.at[step - 1],
                target,
            )
        )
    far_copies = [
        remote(
            cot_ref,
            cot_all.at[me],
            far_s.at[step - 1],
            far_r.at[step - 1],
            ((far + step) % fars) * 4 + near * 2 + core,
        )
        for step in range(1, fars)
    ]
    near_copies = [remote(cot_ref, cot_all.at[me], near_s.at[0], near_r.at[0], beside)]
    core_copies = [remote(cot_ref, cot_all.at[me], core_s.at[0], core_r.at[0], sibling)]
    for copy in swap_copies:
        copy.wait_recv()
    keep_row.wait()
    row_pair = pair(recv_all, recv_far, 2 * fars)
    load.wait()
    hidden = recv_all[...].reshape(n * tokens, hidden_units)
    ocore = []
    for at in range(CHUNKS):
        out = lax.dot_general(
            hidden,
            held[at * chunk : (at + 1) * chunk, :],
            (((1,), (1,)), ((), ())),
            preferred_element_type=jnp.float32,
        )
        part[at] = out.astype(jnp.bfloat16).reshape(fars, 2, 2, tokens, chunk)
        ocore.append(
            remote(
                part.at[at, :, :, 1 - core],
                core_buf.at[at],
                ocore_s.at[at],
                ocore_r.at[at],
                sibling,
            )
        )

    blocks = [me]
    pairs = [pair(cot_ref.at[:, columns_there], cot_far.at[me], 0)]
    for step in range(1, fars):
        far_copies[step - 1].wait_recv()
        block = ((far - step + fars) % fars) * 4 + near * 2 + core
        ref = cot_all.at[block]
        near_copies.append(remote(ref, ref, near_s.at[step], near_r.at[step], beside))
        core_copies.append(remote(ref, ref, core_s.at[step], core_r.at[step], sibling))
        pairs.append(pair(ref.at[:, columns_there], cot_far.at[block], step))
        blocks.append(block)

    onear = []
    for at in range(CHUNKS):
        ocore[at].wait_recv()
        core_sum[at] = added(part[at, :, :, core], core_buf[at])
        onear.append(
            remote(
                core_sum.at[at, :, 1 - near],
                near_buf.at[at],
                onear_s.at[at],
                onear_r.at[at],
                beside,
            )
        )

    for step in range(fars):
        near_copies[step].wait_recv()
        block = ((far - step + fars) % fars) * 4 + (1 - near) * 2 + core
        ref = cot_all.at[block]
        at = fars + step
        core_copies.append(remote(ref, ref, core_s.at[at], core_r.at[at], sibling))
        pairs.append(pair(ref.at[:, columns_there], cot_far.at[block], at))
        blocks.append(block)

    ofar = []

    def push(at):
        onear[at].wait_recv()
        near_sum[at] = added(core_sum[at, :, near], near_buf[at])
        for step in range(1, fars):
            target = (far + step) % fars
            slot = at * (fars - 1) + step - 1
            ofar.append(
                remote(
                    near_sum.at[at, target],
                    far_buf.at[at, step - 1],
                    ofar_s.at[slot],
                    ofar_r.at[slot],
                    target * 4 + near * 2 + core,
                )
            )

    for at in range(CHUNKS // 2):
        push(at)
    for copy in core_copies:
        copy.wait_recv()
    keep_cot.wait()
    tile = hidden_units // 3 if hidden_units % 384 == 0 else hidden_units

    @pl.loop(0, hidden_units // tile)
    def _(at):
        columns = pl.ds(pl.multiple_of(at * tile, tile), tile)
        found = jnp.dot(
            cot_all[...].reshape(n * tokens, width),
            held[:, columns],
            preferred_element_type=jnp.float32,
        )
        grad[:, :, columns] = found.astype(jnp.bfloat16).reshape(n, tokens, tile)

    keep_grad = pltpu.make_async_copy(grad.at[me], back_ref.at[me], own_sem.at[3])
    keep_grad.start()
    oswap = []
    for step in range(1, n):
        target = (me + step) % n
        oswap.append(
            remote(
                grad.at[target],
                back_ref.at[me],
                oswap_s.at[step - 1],
                oswap_r.at[step - 1],
                target,
            )
        )
    for at in range(CHUNKS // 2, CHUNKS):
        push(at)
    passes = []
    for at in range(2 * fars):
        pairs[at].wait_recv()
        ref = cot_far.at[blocks[at]]
        passes.append(remote(ref, ref, pass_s.at[at], pass_r.at[at], sibling))
    for at in range(CHUNKS):
        for step in range(1, fars):
            ofar[at * (fars - 1) + step - 1].wait_recv()
        total = near_sum[at, far].astype(jnp.float32)
        for step in range(1, fars):
            total = total + far_buf[at, step - 1].astype(jnp.float32)
        mixed_ref[:, at * chunk : (at + 1) * chunk] = total.astype(jnp.bfloat16)
    for copy in oswap + passes + [row_pair]:
        copy.wait_recv()
    for copy in far_copies + near_copies + core_copies + swap_copies:
        copy.wait_send()
    for copy in ocore + onear + ofar + oswap + pairs + passes + [row_pair]:
        copy.wait_send()
    keep_grad.wait()


def layer(cot, send, weight):
    n, tokens, hidden_units = send.shape
    width = cot.shape[1]
    chunk = width // CHUNKS
    fars = n // 4
    kind = cot.dtype
    dma = pltpu.SemaphoreType.DMA
    in_vmem = pl.BlockSpec(memory_space=pltpu.VMEM)
    return pl.pallas_call(
        functools.partial(layer_kernel, n),
        out_shape=(
            jax.ShapeDtypeStruct((n, tokens, width), kind),
            jax.ShapeDtypeStruct((n, tokens, hidden_units), kind),
            jax.ShapeDtypeStruct((tokens, width), kind),
            jax.ShapeDtypeStruct((n, tokens, hidden_units), kind),
            jax.ShapeDtypeStruct((n, tokens, width // 2), kind),
            jax.ShapeDtypeStruct((n, tokens, hidden_units), kind),
        ),
        in_specs=[in_vmem, in_vmem, pl.BlockSpec(memory_space=pltpu.HBM)],
        out_specs=[in_vmem] * 6,
        scratch_shapes=[
            pltpu.VMEM(weight.shape, kind),
            pltpu.VMEM((CHUNKS, fars, 2, 2, tokens, chunk), kind),
            pltpu.VMEM((n, tokens, hidden_units), kind),
            pltpu.VMEM((CHUNKS, fars, 2, tokens, chunk), kind),
            pltpu.VMEM((CHUNKS, fars, 2, tokens, chunk), kind),
            pltpu.VMEM((CHUNKS, fars, tokens, chunk), kind),
            pltpu.VMEM((CHUNKS, fars, tokens, chunk), kind),
            pltpu.VMEM((CHUNKS, fars - 1, tokens, chunk), kind),
            dma((4,)),
        ]
        + [dma((fars - 1,))] * 2
        + [dma((fars,))] * 2
        + [dma((2 * fars,))] * 2
        + [dma((n - 1,))] * 2
        + [dma((CHUNKS * (fars - 1),))] * 2
        + [dma((CHUNKS,))] * 4
        + [dma((n - 1,))] * 2
        + [dma((2 * fars + 1,))] * 2
        + [dma((2 * fars,))] * 2,
        compiler_params=pltpu.CompilerParams(
            collective_id=0, has_side_effects=True, vmem_limit_bytes=40 * 1024 * 1024
        ),
    )(cot, send, weight)


def on_device(preactivations, route_weights, expert_ids, down_proj, output_cotangent):
    token_count, per_token, pre_width = preactivations.shape
    hidden_units = pre_width // 2
    model_width = output_cotangent.shape[1]
    experts = lax.axis_size("expert")
    copies = lax.axis_size("dp")
    slot_count = token_count * per_token
    flat_ids = expert_ids.reshape(slot_count)
    slot_token = lax.iota(jnp.int32, slot_count) // per_token
    target = flat_ids * token_count + slot_token
    placement = (
        lax.iota(jnp.int32, experts * token_count)[:, None] == target[None, :]
    ).astype(jnp.bfloat16)
    pre_vals = preactivations.reshape(slot_count, pre_width).astype(jnp.float32)
    gate_pre = pre_vals[:, :hidden_units]
    up_pre = pre_vals[:, hidden_units:]
    sigmoid_gate = jax.nn.sigmoid(gate_pre)
    activated = gate_pre * sigmoid_gate
    hidden = activated * up_pre
    slot_weight = route_weights.reshape(slot_count, 1)
    weighted = (slot_weight * hidden).astype(jnp.bfloat16)
    weight = down_proj[0]

    send = jnp.dot(placement, weighted, preferred_element_type=jnp.float32).astype(jnp.bfloat16)
    send = send.reshape(experts, token_count, hidden_units)
    by_kernel = copies == 2 and experts % 4 == 0 and experts > 4
    rows = experts * token_count
    if by_kernel:
        cot_rows, recv, mixed, grad_back, cot_other, hidden_other = layer(
            output_cotangent, send, weight
        )
        cot_other = cot_other.reshape(rows, model_width // 2)
        hidden_other = hidden_other.reshape(rows, hidden_units)
        cot_rows = cot_rows.reshape(rows, model_width)
        hidden_rows = recv.reshape(rows, hidden_units)
    else:
        cot_rows = lax.all_gather(output_cotangent, "expert", axis=0, tiled=True)
        recv = lax.all_to_all(send, "expert", split_axis=0, concat_axis=0, tiled=True)
        hidden_rows = recv.reshape(rows, hidden_units)
        grad_rows = (
            jnp.dot(cot_rows, weight, preferred_element_type=jnp.float32)
            .astype(jnp.bfloat16)
            .reshape(experts, token_count, hidden_units)
        )
        mixed_part = lax.dot_general(
            hidden_rows, weight, (((1,), (1,)), ((), ())), preferred_element_type=jnp.float32
        ).astype(jnp.bfloat16)
        mixed = lax.psum_scatter(mixed_part, "expert", scatter_dimension=0, tiled=True)
        grad_back = lax.all_to_all(grad_rows, "expert", split_axis=0, concat_axis=0, tiled=True)
    grad_back = grad_back.reshape(rows, hidden_units)

    if by_kernel:
        half = model_width // 2
        cot_keep = lax.dynamic_slice_in_dim(cot_rows, lax.axis_index("dp") * half, half, 1)
        contract = (((0,), (0,)), ((), ()))
        weight_grads = lax.dot_general(
            cot_keep, hidden_rows, contract, preferred_element_type=jnp.float32
        ) + lax.dot_general(
            cot_other, hidden_other, contract, preferred_element_type=jnp.float32
        )
    else:
        weight_grads = lax.psum_scatter(
            lax.dot_general(
                cot_rows, hidden_rows, (((0,), (0,)), ((), ())), preferred_element_type=jnp.float32
            ).astype(jnp.bfloat16),
            "dp",
            scatter_dimension=0,
            tiled=True,
        ).astype(jnp.float32)

    slot_grad = lax.dot_general(
        placement, grad_back, (((0,), (0,)), ((), ())), preferred_element_type=jnp.float32
    )
    route_grads = jnp.sum(slot_grad * hidden, axis=1).reshape(token_count, per_token)
    hidden_grad = slot_weight * slot_grad
    gate_grad = hidden_grad * up_pre * (sigmoid_gate * (1.0 + gate_pre * (1.0 - sigmoid_gate)))
    up_grad = hidden_grad * activated
    pre_grads = (
        jnp.concatenate([gate_grad, up_grad], axis=1)
        .astype(jnp.bfloat16)
        .reshape(token_count, per_token, pre_width)
    )
    return (mixed, route_grads, pre_grads, weight_grads[None])


def solution(mesh):
    in_specs = (
        P(("dp", "expert"), None, None),
        P(("dp", "expert"), None),
        P(("dp", "expert"), None),
        P("expert", None, None),
        P(("dp", "expert"), None),
    )
    out_specs = (
        P(("dp", "expert"), None),
        P(("dp", "expert"), None),
        P(("dp", "expert"), None, None),
        P("expert", "dp", None),
    )
    return jax.shard_map(
        on_device, mesh=mesh, in_specs=in_specs, out_specs=out_specs, check_vma=False
    )
```
